32 devices in a mesh: ky: 8 (over y, x, core), kz: 4 (over z).
Axes of the slice: x: 2, y: 2, z: 4, core: 2. Of those that a mesh axis runs over, the one named last changes fastest.
Arguments:
- fields: bfloat16 [4, 2, 8, 1024, 1024], P(None, None, None, 'ky', 'kz'), may hold values from -6 to 6
- offsets: int32 [8], replicated, may hold values from 0 to 1023, as said below
Outputs:
- velocity_field: bfloat16 [3, 2, 8, 1024, 1024], P(None, None, 'ky', 'kz')
- scalar_spectrum: bfloat16 [2, 8, 1024, 1024], P(None, None, 'ky', 'kz')
The draws below stay inside these ranges and needn't reach their ends.
Inputs may be any that keep to these rules, and one draw needn't show every extreme that they name: `offsets`: ky roll of each kx plane; both ends are taken in every draw.
All inputs are finite; a program needn't handle non-finite values.
Results may differ from the reference program's by a relative error of at most 0.0059.
Values may be sent and summed in bfloat16 or wider, within the bound.
No kernel may reach another device: no remote copies, remote signals or barrier semaphores. Data moves between devices by JAX's collectives and lax.ppermute only.
A program may use at most 128 MiB of HBM per device.

```python
import math
import jax
import jax.numpy as jnp
from jax import lax

KY = 1024
KZ = 1024
KX = 8


def draw_offsets(key, part):
    key_values, key_top, key_low = jax.random.split(key, 3)
    values = jax.random.randint(key_values, (KX,), 0, KY, dtype=jnp.int32)
    top_slot = jax.random.randint(key_top, (), 0, KX, dtype=jnp.int32)
    low_slot = (top_slot + 1 + jax.random.randint(key_low, (), 0, KX - 1, dtype=jnp.int32)) % KX
    values = values.at[top_slot].set(KY - 1)
    values = values.at[low_slot].set(0)
    return values


def level_of(rng, dims, pieces, least, largest):
    level = 1.0
    for position, parts in pieces:
        steps = jax.random.uniform(jax.random.fold_in(jax.random.fold_in(rng, 6), position), (parts,), jnp.float32, least / len(pieces), largest / len(pieces))
        level = level * jnp.repeat(jnp.exp(steps), dims[position] // parts).reshape((-1,) + (1,) * (len(dims) - 1 - position))
    return level


def scatter_about(rng, extent, scale, limit, cuts=(), held_as=jnp.bfloat16):
    result = jax.random.normal(rng, extent, jnp.float32) * scale
    if len(cuts) > 0:
        result = level_of(rng, extent, cuts, -0.22, 0.18) * result
    return jnp.clip(result, min=-limit, max=limit).astype(held_as)


def setup_inputs(seed: int = 0) -> dict:
    key_list = jax.random.split(jax.random.key(seed), 3)
    fields = scatter_about(key_list[0], (4, 2, KX, KY, KZ), 1.0, 6.0, ((3, 8), (4, 4)))
    offsets = draw_offsets(jax.random.fold_in(key_list[2], 71), 0)
    return dict(fields=fields, offsets=offsets)


def tables(length):
    counter = jnp.arange(length, dtype=jnp.int32)
    product = counter[:, None] * counter[None, :] % length
    angles = product.astype(jnp.float32) * (2.0 * math.pi / length)
    return (jnp.cos(angles).astype(jnp.bfloat16), jnp.sin(angles).astype(jnp.bfloat16))

def inverse(values, pattern, length):
    cos_table, sin_table = tables(length)

    def apply_table(operand, table):
        return jnp.einsum(pattern, operand.astype(jnp.float32), table.astype(jnp.float32), precision=lax.Precision.HIGHEST)
    real_part = values[:, 0]
    imag_part = values[:, 1]
    out_real = apply_table(real_part, cos_table) - apply_table(imag_part, sin_table)
    out_imag = apply_table(real_part, sin_table) + apply_table(imag_part, cos_table)
    factor = 1.0 / math.sqrt(length)
    return (jnp.stack([out_real, out_imag], axis=1) * factor).astype(jnp.bfloat16)

def reference(fields, offsets):
    rolled = jax.vmap(lambda kx_plane, amount: jnp.roll(kx_plane, amount, axis=2), in_axes=(2, 0), out_axes=2)(fields, offsets)

    def transform(component):
        along_y = inverse(component[None], 'cxkz,ky->cxyz', KY)
        return inverse(along_y, 'cxyk,kz->cxyz', KZ)[0]
    velocity_field = lax.map(transform, rolled[:3])
    return (velocity_field, rolled[3])
```

```python
import functools
import math

import jax
import jax.numpy as jnp
import ml_dtypes
import numpy as np
from jax import lax
from jax.experimental import pallas as pl
from jax.experimental.pallas import tpu as pltpu
from jax.sharding import PartitionSpec as P

VMEM_LIMIT = 40 * 1024 * 1024


def tables(length):
    counter = np.arange(length, dtype=np.int64)
    product = (counter[:, None] * counter[None, :]) % length
    angles = product.astype(np.float32) * np.float32(2.0 * math.pi / length)
    return (
        jnp.asarray(np.cos(angles).astype(ml_dtypes.bfloat16)),
        jnp.asarray(np.sin(angles).astype(ml_dtypes.bfloat16)),
    )


def dot(left, right):
    return lax.dot_general(left, right, (((1,), (0,)), ((), ())), preferred_element_type=jnp.float32)


def shift_rows(blocks_ref, offset, store):
    count, _, rows, _ = blocks_ref.shape
    whole, rest = offset // rows, offset % rows
    to_row = lax.broadcasted_iota(jnp.int32, (rows, 2 * rows), 0)
    from_row = lax.broadcasted_iota(jnp.int32, (rows, 2 * rows), 1)
    pick = jnp.where(from_row == rows + to_row - rest, 1.0, 0.0).astype(jnp.bfloat16)
    for block in range(count):
        here = lax.rem(block - whole + count, count)
        before = lax.rem(block - whole - 1 + 2 * count, count)
        for part in range(2):
            window = jnp.concatenate([blocks_ref[before, part], blocks_ref[here, part]], axis=0)
            store(block, part, dot(pick, window).astype(jnp.bfloat16))


def y_kernel(place_ref, blocks_ref, cos_ref, sin_ref, *refs):
    outs, rolled = refs[:-1], refs[-1]
    step = pl.program_id(0)
    _, _, rows, columns = blocks_ref.shape
    factor = 1.0 / math.sqrt(cos_ref.shape[1])

    @pl.when(step == 0)
    def _():
        def store(block, part, values):
            rolled[pl.ds(block * rows, rows), pl.ds(part * columns, columns)] = values

        shift_rows(blocks_ref, place_ref[0], store)

    by_cos = dot(cos_ref[...], rolled[...])
    by_sin = dot(sin_ref[...], rolled[...])
    real = ((by_cos[:, :columns] - by_sin[:, columns:]) * factor).astype(jnp.bfloat16)
    imag = ((by_sin[:, :columns] + by_cos[:, columns:]) * factor).astype(jnp.bfloat16)
    for index, out in enumerate(outs):

        @pl.when(step == index)
        def _(out=out):
            out[0] = real
            out[1] = imag


def y_transform(blocks, place, cos_table, sin_table, targets):
    count, _, rows, columns = blocks.shape
    length = count * rows
    y_rows = length // targets

    def table_rows(step, place_ref):
        return (lax.rem(place_ref[1] + step, targets), 0)

    whole = pl.BlockSpec((2, y_rows, columns), lambda step, place_ref: (0, 0, 0))
    return pl.pallas_call(
        y_kernel,
        out_shape=[jax.ShapeDtypeStruct((2, y_rows, columns), jnp.bfloat16)] * targets,
        grid_spec=pltpu.PrefetchScalarGridSpec(
            num_scalar_prefetch=1,
            grid=(targets,),
            in_specs=[
                pl.BlockSpec(blocks.shape, lambda step, place_ref: (0, 0, 0, 0)),
                pl.BlockSpec((y_rows, length), table_rows),
                pl.BlockSpec((y_rows, length), table_rows),
            ],
            out_specs=[whole] * targets,
            scratch_shapes=[pltpu.VMEM((length, 2 * columns), jnp.bfloat16)],
        ),
        compiler_params=pltpu.CompilerParams(vmem_limit_bytes=VMEM_LIMIT),
        cost_estimate=pl.CostEstimate(
            flops=8 * length * length * columns, bytes_accessed=8 * length * length, transcendentals=0
        ),
        name="y_transform",
    )(place, blocks, cos_table, sin_table)


def z_kernel(targets, place_ref, *refs):
    pieces = refs[:targets]
    cos_ref, sin_ref = refs[targets : targets + 2]
    out, joined = refs[-2:]
    _, rows, columns = pieces[0].shape
    factor = 1.0 / math.sqrt(cos_ref.shape[0])

    @pl.when(pl.program_id(0) == 0)
    def _():
        for step, piece in enumerate(pieces):
            source = lax.rem(place_ref[1] + targets - step, targets)
            start = pl.multiple_of(source * columns, columns)
            for part in range(2):
                joined[pl.ds(part * rows, rows), pl.ds(start, columns)] = piece[part]

    by_cos = dot(joined[...], cos_ref[...])
    by_sin = dot(joined[...], sin_ref[...])
    out[0, 0, 0] = ((by_cos[:rows] - by_sin[rows:]) * factor).astype(jnp.bfloat16)
    out[0, 1, 0] = ((by_sin[:rows] + by_cos[rows:]) * factor).astype(jnp.bfloat16)


def z_transform(pieces, place, cos_table, sin_table, component, components, field):
    targets = len(pieces)
    _, rows, columns = pieces[0].shape
    length = columns * targets
    tile = 256
    piece = pl.BlockSpec(pieces[0].shape, lambda step, place_ref: (0, 0, 0))
    table = pl.BlockSpec((length, tile), lambda step, place_ref: (0, step))
    in_specs = [piece] * targets + [table] * 2
    operands = [place, *pieces, cos_table, sin_table]
    aliases = {}
    if field is not None:
        in_specs.append(pl.BlockSpec(memory_space=pl.ANY))
        operands.append(field)
        aliases = {len(operands) - 1: 0}
    return pl.pallas_call(
        functools.partial(z_kernel, targets),
        out_shape=jax.ShapeDtypeStruct((components, 2, 1, rows, length), jnp.bfloat16),
        grid_spec=pltpu.PrefetchScalarGridSpec(
            num_scalar_prefetch=1,
            grid=(length // tile,),
            in_specs=in_specs,
            out_specs=pl.BlockSpec((1, 2, 1, rows, tile), lambda step, place_ref: (component, 0, 0, 0, step)),
            scratch_shapes=[pltpu.VMEM((2 * rows, length), jnp.bfloat16)],
        ),
        input_output_aliases=aliases,
        compiler_params=pltpu.CompilerParams(vmem_limit_bytes=VMEM_LIMIT),
        cost_estimate=pl.CostEstimate(
            flops=8 * rows * length * length, bytes_accessed=8 * length * length, transcendentals=0
        ),
        name="z_transform",
    )(*operands)


def roll_kernel(place_ref, blocks_ref, out):
    def store(block, part, values):
        out[block, part] = values

    shift_rows(blocks_ref, place_ref[0], store)


def roll_plane(blocks, place):
    whole = pl.BlockSpec(blocks.shape, lambda step, place_ref: (0, 0, 0, 0))
    return pl.pallas_call(
        roll_kernel,
        out_shape=jax.ShapeDtypeStruct(blocks.shape, jnp.bfloat16),
        grid_spec=pltpu.PrefetchScalarGridSpec(
            num_scalar_prefetch=1, grid=(1,), in_specs=[whole], out_specs=whole
        ),
        compiler_params=pltpu.CompilerParams(vmem_limit_bytes=VMEM_LIMIT),
        cost_estimate=pl.CostEstimate(
            flops=4 * blocks.size * blocks.shape[2], bytes_accessed=4 * blocks.size, transcendentals=0
        ),
        name="roll_plane",
    )(place, blocks)


def to_planes(component):
    return lax.all_to_all(component.transpose(1, 0, 2, 3), "ky", 0, 0, tiled=True)


def shards(fields, offsets):
    components = fields.shape[0] - 1
    targets = lax.axis_size("kz")
    assert fields.shape[2] == lax.axis_size("ky")
    place = jnp.stack([offsets[lax.axis_index("ky")], lax.axis_index("kz").astype(jnp.int32)])
    y_tables = tables(fields.shape[3] * lax.axis_size("ky"))
    z_tables = tables(fields.shape[4] * targets)
    field = None
    for component in range(components):
        blocks = to_planes(fields[component])
        own, *others = y_transform(blocks, place, *y_tables, targets)
        pieces = [own]
        for step, piece in enumerate(others, 1):
            pairs = [(i, (i + step) % targets) for i in range(targets)]
            pieces.append(lax.ppermute(piece, "kz", pairs))
        field = z_transform(pieces, place, *z_tables, component, components, field)
    plane = roll_plane(to_planes(fields[components]), place)
    scalar = lax.all_to_all(plane, "ky", 0, 0, tiled=True).transpose(1, 0, 2, 3)
    return (field, scalar)


def solution(mesh):
    placed = (P(None, None, None, "ky", "kz"), P())
    return jax.shard_map(
        shards,
        mesh=mesh,
        in_specs=placed,
        out_specs=(P(None, None, "ky", "kz", None), P(None, None, "ky", "kz")),
        check_vma=False,
    )
```

```python
import functools
import math

import jax
import jax.numpy as jnp
import ml_dtypes
import numpy as np
from jax import lax
from jax.experimental import pallas as pl
from jax.experimental.pallas import tpu as pltpu
from jax.sharding import PartitionSpec as P

VMEM_LIMIT = 64 * 1024 * 1024
COST = pl.CostEstimate(flops=0, bytes_accessed=0, transcendentals=0)
HIGH = pl.CostEstimate(flops=40_000_000_000, bytes_accessed=0, transcendentals=0)


def tables(length):
    counter = np.arange(length, dtype=np.int64)
    product = (counter[:, None] * counter[None, :]) % length
    angles = product.astype(np.float32) * np.float32(2.0 * math.pi / length)
    return (np.cos(angles).astype(ml_dtypes.bfloat16), np.sin(angles).astype(ml_dtypes.bfloat16))


def y_table(length, targets):
    order = np.concatenate([np.arange(0, length, 2), np.arange(1, length, 2)])
    parts = [table[: length // 2, order].reshape(targets // 2, length // targets, length) for table in tables(length)]
    return jnp.asarray(np.concatenate(parts, axis=1))


def z_table(length, tile):
    half = length // 2
    order = np.concatenate([np.arange(0, length, 2), np.arange(1, length, 2)])
    parts = [table[order, :half].reshape(length, half // tile, tile).swapaxes(0, 1) for table in tables(length)]
    return jnp.asarray(np.concatenate(parts, axis=2))


def dot(left, right):
    return lax.dot_general(left, right, (((1,), (0,)), ((), ())), preferred_element_type=jnp.float32)


def shift_rows(slots, offset, store, parity):
    count, rows, _ = slots[0].shape
    whole, rest = offset // rows, offset % rows
    to_row = lax.broadcasted_iota(jnp.int32, (rows, 2 * rows), 0)
    if parity:
        to_row = jnp.where(to_row < rows // 2, 2 * to_row, 2 * to_row - (rows - 1))
    from_row = lax.broadcasted_iota(jnp.int32, (rows, 2 * rows), 1)
    pick = jnp.where(from_row == rows + to_row - rest, 1.0, 0.0).astype(jnp.bfloat16)
    for block in range(count):
        here = lax.rem(block - whole + count, count)
        before = lax.rem(block - whole - 1 + 2 * count, count)
        for part, slot in enumerate(slots):
            window = jnp.concatenate([slot[before], slot[here]], axis=0)
            store(block, part, dot(pick, window).astype(jnp.bfloat16))


def y_kernel(targets, halves, place_ref, blocks_hbm, table_hbm, *refs):
    count = targets * halves
    outs, (blocks, table, rolled, pieces, sems, out_sems) = refs[:count], refs[count:]
    planes, _, rows, columns = blocks.shape
    length = planes * rows
    y_rows = length // targets
    half_rows = y_rows // halves
    pairs = targets // 2
    factor = 1.0 / math.sqrt(length)

    load = pltpu.make_async_copy(blocks_hbm.at[:, pl.ds(0, 2)], blocks, sems.at[pairs])
    load.start()
    loads = []
    for step in range(pairs):
        wanted = lax.rem(place_ref[1] + step, pairs)
        loads.append(pltpu.make_async_copy(table_hbm.at[wanted], table.at[step], sems.at[step]))
        loads[-1].start()
    load.wait()

    def store(block, part, values):
        lanes = pl.ds(part * columns, columns)
        for odd in range(2):
            start = odd * (length // 2) + block * (rows // 2)
            rolled[pl.ds(start, rows // 2), lanes] = values[odd * (rows // 2) : (odd + 1) * (rows // 2)]

    shift_rows([blocks.at[:, part] for part in range(2)], place_ref[0], store, parity=True)

    def product(step, start):
        both = dot(table[step, :, pl.ds(start, length // 2)], rolled[pl.ds(start, length // 2), :])
        real = both[:y_rows, :columns] - both[y_rows:, columns:]
        imag = both[y_rows:, :columns] + both[:y_rows, columns:]
        return real, imag

    stores = []
    for step in range(pairs):
        loads[step].wait()
        sign = jnp.where(lax.rem(place_ref[1] + step, targets) < pairs, factor, -factor)
        even = product(step, 0)
        odd = product(step, length // 2)
        for part in range(2):
            from_even, from_odd = even[part] * factor, odd[part] * sign
            pieces[step, part] = (from_even + from_odd).astype(jnp.bfloat16)
            pieces[step + pairs, part] = (from_even - from_odd).astype(jnp.bfloat16)
        for index in (step, step + pairs):
            for half in range(halves):
                number = half * targets + index
                stores.append(
                    pltpu.make_async_copy(
                        pieces.at[index, :, pl.ds(half * half_rows, half_rows)], outs[number], out_sems.at[number]
                    )
                )
                stores[-1].start()
    for copy in stores:
        copy.wait()


IN_HBM = pl.BlockSpec(memory_space=pltpu.HBM)
IN_SMEM = pl.BlockSpec(memory_space=pltpu.SMEM)


def y_transform(blocks, place, table, targets, halves, cost):
    planes, _, rows, columns = blocks.shape
    length = planes * rows
    y_rows = length // targets
    count = targets * halves
    return pl.pallas_call(
        functools.partial(y_kernel, targets, halves),
        out_shape=[jax.ShapeDtypeStruct((2, y_rows // halves, columns), jnp.bfloat16)] * count,
        in_specs=[IN_SMEM, IN_HBM, IN_HBM],
        out_specs=[IN_HBM] * count,
        scratch_shapes=[
            pltpu.VMEM((planes, 2, rows, columns), jnp.bfloat16),
            pltpu.VMEM(table.shape, jnp.bfloat16),
            pltpu.VMEM((length, 2 * columns), jnp.bfloat16),
            pltpu.VMEM((targets, 2, y_rows, columns), jnp.bfloat16),
            pltpu.SemaphoreType.DMA((targets // 2 + 1,)),
            pltpu.SemaphoreType.DMA((count,)),
        ],
        compiler_params=pltpu.CompilerParams(vmem_limit_bytes=VMEM_LIMIT),
        cost_estimate=cost,
        name="y_transform",
    )(place, blocks, table)


def z_kernel(layout, targets, component, first_row, place_ref, *refs):
    pieces, table_hbm = refs[: len(layout)], refs[len(layout)]
    field, joined, split, table, out, sems, table_sems, out_sems = refs[-8:]
    rows = joined.shape[0] // 2
    tiles, length, tile = table.shape[0], table.shape[1], table.shape[2] // 2
    columns = length // targets
    factor = 1.0 / math.sqrt(length)

    def place_piece(number):
        piece, (behind, row, lane) = pieces[number], layout[number]
        source = lax.rem(place_ref[1] + targets - behind, targets)
        _, some_rows, some_columns = piece.shape
        start = pl.multiple_of(source * columns, columns) + lane
        return [
            pltpu.make_async_copy(
                piece.at[part],
                joined.at[pl.ds(part * rows + row, some_rows), pl.ds(start, some_columns)],
                sems.at[number, part],
            )
            for part in range(2)
        ]

    loads = [copy for number in range(len(layout)) for copy in place_piece(number)]
    for copy in loads:
        copy.start()
    tables = [pltpu.make_async_copy(table_hbm.at[step], table.at[step], table_sems.at[step]) for step in range(tiles)]
    for copy in tables:
        copy.start()

    lane = lax.broadcasted_iota(jnp.int32, (columns, columns), 1)
    wanted = jnp.where(lane < columns // 2, 2 * lane, 2 * lane - (columns - 1))
    pick = jnp.where(lax.broadcasted_iota(jnp.int32, (columns, columns), 0) == wanted, 1.0, 0.0).astype(jnp.bfloat16)
    for copy in loads:
        copy.wait()
    for source in range(targets):
        parted = dot(joined[:, pl.ds(source * columns, columns)], pick).astype(jnp.bfloat16)
        split[:, pl.ds(source * columns // 2, columns // 2)] = parted[:, : columns // 2]
        split[:, pl.ds((length + source * columns) // 2, columns // 2)] = parted[:, columns // 2 :]

    def product(step, start):
        lanes = pl.ds(start, length // 2)
        both = dot(split[:, lanes], table[step, lanes, :])
        return both[:rows, :tile] - both[rows:, tile:], both[:rows, tile:] + both[rows:, :tile]

    stores = []
    for step in range(tiles):
        tables[step].wait()
        even = product(step, 0)
        odd = product(step, length // 2)
        for part in range(2):
            out[step, part] = ((even[part] + odd[part]) * factor).astype(jnp.bfloat16)
            out[step + tiles, part] = ((even[part] - odd[part]) * factor).astype(jnp.bfloat16)
        for number in (step, step + tiles):
            stores.append(
                pltpu.make_async_copy(
                    out.at[number],
                    field.at[component, :, 0, pl.ds(first_row, rows), pl.ds(number * tile, tile)],
                    out_sems.at[number],
                )
            )
            stores[-1].start()
    for copy in stores:
        copy.wait()


def z_transform(pieces, layout, place, table, targets, component, first_row, field, shape, cost):
    rows = max(row + piece.shape[1] for piece, (_, row, _) in zip(pieces, layout))
    tiles, length, _ = table.shape
    through = [] if field is None else [field]
    return pl.pallas_call(
        functools.partial(z_kernel, layout, targets, component, first_row),
        out_shape=jax.ShapeDtypeStruct(shape, jnp.bfloat16),
        in_specs=[IN_SMEM] + [IN_HBM] * (len(pieces) + 1 + len(through)),
        out_specs=IN_HBM,
        scratch_shapes=[
            pltpu.VMEM((2 * rows, length), jnp.bfloat16),
            pltpu.VMEM((2 * rows, length), jnp.bfloat16),
            pltpu.VMEM(table.shape, jnp.bfloat16),
            pltpu.VMEM((2 * tiles, 2, rows, length // tiles // 2), jnp.bfloat16),
            pltpu.SemaphoreType.DMA((len(pieces), 2)),
            pltpu.SemaphoreType.DMA((tiles,)),
            pltpu.SemaphoreType.DMA((2 * tiles,)),
        ],
        input_output_aliases={} if field is None else {len(pieces) + 2: 0},
        compiler_params=pltpu.CompilerParams(vmem_limit_bytes=VMEM_LIMIT),
        cost_estimate=cost,
        name="z_transform",
    )(place, *pieces, table, *through)


def roll_kernel(numbers, place_ref, *refs):
    slots = refs[: len(numbers)]
    out_hbm, blocks, out, sems, out_sem = refs[len(numbers) :]
    loads = [
        pltpu.make_async_copy(slot.at[:, number], blocks.at[part], sems.at[part])
        for part, (slot, number) in enumerate(zip(slots, numbers))
    ]
    for copy in loads:
        copy.start()
    for copy in loads:
        copy.wait()

    def store(block, part, values):
        out[block, part] = values

    shift_rows([blocks.at[part] for part in range(len(numbers))], place_ref[0], store, parity=False)
    copy = pltpu.make_async_copy(out, out_hbm, out_sem.at[0])
    copy.start()
    copy.wait()


def roll_planes(place, *slots):
    count, _, rows, columns = slots[0][0].shape
    return pl.pallas_call(
        functools.partial(roll_kernel, [number for _, number in slots]),
        out_shape=jax.ShapeDtypeStruct((count, len(slots), rows, columns), jnp.bfloat16),
        in_specs=[IN_SMEM] + [IN_HBM] * len(slots),
        out_specs=IN_HBM,
        scratch_shapes=[
            pltpu.VMEM((len(slots), count, rows, columns), jnp.bfloat16),
            pltpu.VMEM((count, len(slots), rows, columns), jnp.bfloat16),
            pltpu.SemaphoreType.DMA((len(slots),)),
            pltpu.SemaphoreType.DMA((1,)),
        ],
        compiler_params=pltpu.CompilerParams(vmem_limit_bytes=VMEM_LIMIT),
        cost_estimate=COST,
        name="roll_planes",
    )(place, *[blocks for blocks, _ in slots])


def restack_kernel(steps, from_hbm, out_hbm, held, sems, out_sems):
    loads = [pltpu.make_async_copy(from_hbm.at[source], held.at[part], sems.at[part]) for part, (source, _) in enumerate(steps)]
    for copy in loads:
        copy.start()
    stores = []
    for part, (_, target) in enumerate(steps):
        loads[part].wait()
        stores.append(pltpu.make_async_copy(held.at[part], out_hbm.at[target], out_sems.at[part]))
        stores[-1].start()
    for copy in stores:
        copy.wait()


def restack(array, steps, shape, name):
    return pl.pallas_call(
        functools.partial(restack_kernel, steps),
        out_shape=jax.ShapeDtypeStruct(shape, array.dtype),
        in_specs=[IN_HBM],
        out_specs=IN_HBM,
        scratch_shapes=[
            pltpu.VMEM((len(steps), array.shape[-3] if array.ndim == 5 else array.shape[0], *array.shape[-2:]), array.dtype),
            pltpu.SemaphoreType.DMA((len(steps),)),
            pltpu.SemaphoreType.DMA((len(steps),)),
        ],
        compiler_params=pltpu.CompilerParams(vmem_limit_bytes=VMEM_LIMIT),
        cost_estimate=COST,
        name=name,
    )(array)


def by_plane(fields, *slots):
    _, _, planes, rows, columns = fields.shape
    steps = [(slot, (slice(None), number)) for number, slot in enumerate(slots)]
    return restack(fields, steps, (planes, len(slots), rows, columns), "by_plane")


def by_part(planes):
    count, parts, rows, columns = planes.shape
    steps = [((slice(None), part), (part,)) for part in range(parts)]
    return restack(planes, steps, (parts, count, rows, columns), "by_part")


def nothing_kernel(*refs):
    pass


def after(array, *others, cost=COST):
    anywhere = IN_HBM
    return pl.pallas_call(
        nothing_kernel,
        out_shape=jax.ShapeDtypeStruct(array.shape, array.dtype),
        in_specs=[anywhere] * (1 + len(others)),
        out_specs=anywhere,
        input_output_aliases={0: 0},
        compiler_params=pltpu.CompilerParams(vmem_limit_bytes=VMEM_LIMIT),
        cost_estimate=cost,
        name="after",
    )(array, *others)


def exchange(blocks):
    return lax.all_to_all(blocks, "ky", 0, 0, tiled=True)


def along_z(others):
    targets = len(others) + 1
    return [
        lax.ppermute(piece, "kz", [(i, (i + step) % targets) for i in range(targets)])
        for step, piece in enumerate(others, 1)
    ]


def shards(fields, offsets):
    components = fields.shape[0] - 1
    targets = lax.axis_size("kz")
    assert fields.shape[2] == lax.axis_size("ky") and components == 3
    place = jnp.stack([offsets[lax.axis_index("ky")], lax.axis_index("kz").astype(jnp.int32)])
    y_rows = fields.shape[3] * lax.axis_size("ky") // targets
    shape = (components, 2, 1, y_rows, fields.shape[4] * targets)
    ky_table = y_table(y_rows * targets, targets)
    kz_table = z_table(shape[-1], 256)

    def y_of(blocks, halves, cost=COST):
        pieces = y_transform(blocks, place, ky_table, targets, halves, cost)
        groups = [pieces[half * targets : (half + 1) * targets] for half in range(halves)]
        return [[group[0], *along_z(group[1:])] for group in groups]

    def z_of(groups, starts, component, first_row, field, cost=COST):
        layout = [(behind, *start) for start in starts for behind in range(targets)]
        pieces = [piece for group in groups for piece in group]
        return z_transform(pieces, layout, place, kz_table, targets, component, first_row, field, shape, cost)

    by_rows = [(0, 0), (y_rows // 2, 0)]
    blocks0 = exchange(by_plane(fields, (0, 0), (0, 1)))
    blocks1 = exchange(after(by_plane(fields, (1, 0), (1, 1), (components, 0), (components, 1)), blocks0))
    pieces0 = y_of(blocks0, 1, HIGH)[0]
    pieces1 = y_of(blocks1, 1)[0]
    third = after(by_plane(fields, (2, 0), (2, 1)), blocks1, *pieces0[1:])
    blocks2 = exchange(after(third, pieces1[0], cost=HIGH))
    field = z_of([pieces0], by_rows[:1], 0, 0, None, HIGH)
    pieces2, pieces3 = y_of(after(blocks2, field), 2)
    plane = roll_planes(place, (blocks1, 2), (blocks1, 3))
    scalar = by_part(exchange(plane))
    field = z_of([pieces1], by_rows[:1], 1, 0, field)
    pieces2[0] = after(pieces2[0], plane, cost=HIGH)
    field = z_of([pieces2], by_rows[:1], 2, 0, field, HIGH)
    field = z_of([pieces3], by_rows[:1], 2, y_rows // 2, field)
    return (field, scalar)


def solution(mesh):
    placed = (P(None, None, None, "ky", "kz"), P())
    return jax.shard_map(
        shards,
        mesh=mesh,
        in_specs=placed,
        out_specs=(P(None, None, "ky", "kz", None), P(None, None, "ky", "kz")),
        check_vma=False,
    )
```

```python
import functools
import math

import jax
import jax.numpy as jnp
import ml_dtypes
import numpy as np
from jax import lax
from jax.experimental import pallas as pl
from jax.experimental.pallas import tpu as pltpu
from jax.sharding import PartitionSpec as P

VMEM_LIMIT = 64 * 1024 * 1024
COST = pl.CostEstimate(flops=0, bytes_accessed=0, transcendentals=0)
MID = pl.CostEstimate(flops=8_000_000_000, bytes_accessed=0, transcendentals=0)
HIGH = pl.CostEstimate(flops=40_000_000_000, bytes_accessed=0, transcendentals=0)


def tables(length):
    counter = np.arange(length, dtype=np.int64)
    product = (counter[:, None] * counter[None, :]) % length
    angles = product.astype(np.float32) * np.float32(2.0 * math.pi / length)
    return (np.cos(angles).astype(ml_dtypes.bfloat16), np.sin(angles).astype(ml_dtypes.bfloat16))


def y_table(length, targets):
    order = np.concatenate([np.arange(0, length, 2), np.arange(1, length, 2)])
    parts = [table[: length // 2, order].reshape(targets // 2, length // targets, length) for table in tables(length)]
    return jnp.asarray(np.concatenate(parts, axis=1))


def z_table(length, tile):
    half = length // 2
    order = np.concatenate([np.arange(0, length, 2), np.arange(1, length, 2)])
    parts = [table[order, :half].reshape(length, half // tile, tile).swapaxes(0, 1) for table in tables(length)]
    return jnp.asarray(np.concatenate(parts, axis=2))


def dot(left, right):
    return lax.dot_general(left, right, (((1,), (0,)), ((), ())), preferred_element_type=jnp.float32)


def shift_rows(slots, offset, store, parity):
    count, rows, _ = slots[0].shape
    whole, rest = offset // rows, offset % rows
    to_row = lax.broadcasted_iota(jnp.int32, (rows, 2 * rows), 0)
    if parity:
        to_row = jnp.where(to_row < rows // 2, 2 * to_row, 2 * to_row - (rows - 1))
    from_row = lax.broadcasted_iota(jnp.int32, (rows, 2 * rows), 1)
    pick = jnp.where(from_row == rows + to_row - rest, 1.0, 0.0).astype(jnp.bfloat16)
    for block in range(count):
        here = lax.rem(block - whole + count, count)
        before = lax.rem(block - whole - 1 + 2 * count, count)
        for part, slot in enumerate(slots):
            window = jnp.concatenate([slot[before], slot[here]], axis=0)
            store(block, part, dot(pick, window).astype(jnp.bfloat16))


def y_kernel(targets, halves, place_ref, blocks_hbm, table_hbm, *refs):
    count = targets * halves
    outs, (blocks, table, rolled, pieces, sems, out_sems) = refs[:count], refs[count:]
    planes, _, rows, columns = blocks.shape
    length = planes * rows
    y_rows = length // targets
    half_rows = y_rows // halves
    pairs = targets // 2
    factor = 1.0 / math.sqrt(length)

    load = pltpu.make_async_copy(blocks_hbm.at[:, pl.ds(0, 2)], blocks, sems.at[pairs])
    load.start()
    loads = []
    for step in range(pairs):
        wanted = lax.rem(place_ref[1] + step, pairs)
        loads.append(pltpu.make_async_copy(table_hbm.at[wanted], table.at[step], sems.at[step]))
        loads[-1].start()
    load.wait()

    def store(block, part, values):
        lanes = pl.ds(part * columns, columns)
        for odd in range(2):
            start = odd * (length // 2) + block * (rows // 2)
            rolled[pl.ds(start, rows // 2), lanes] = values[odd * (rows // 2) : (odd + 1) * (rows // 2)]

    shift_rows([blocks.at[:, part] for part in range(2)], place_ref[0], store, parity=True)

    def product(step, start):
        both = dot(table[step, :, pl.ds(start, length // 2)], rolled[pl.ds(start, length // 2), :])
        real = both[:y_rows, :columns] - both[y_rows:, columns:]
        imag = both[y_rows:, :columns] + both[:y_rows, columns:]
        return real, imag

    stores = []
    for step in range(pairs):
        loads[step].wait()
        sign = jnp.where(lax.rem(place_ref[1] + step, targets) < pairs, factor, -factor)
        even = product(step, 0)
        odd = product(step, length // 2)
        for part in range(2):
            from_even, from_odd = even[part] * factor, odd[part] * sign
            pieces[step, part] = (from_even + from_odd).astype(jnp.bfloat16)
            pieces[step + pairs, part] = (from_even - from_odd).astype(jnp.bfloat16)
        for index in (step, step + pairs):
            for half in range(halves):
                number = half * targets + index
                stores.append(
                    pltpu.make_async_copy(
                        pieces.at[index, :, pl.ds(half * half_rows, half_rows)], outs[number], out_sems.at[number]
                    )
                )
                stores[-1].start()
    for copy in stores:
        copy.wait()


IN_HBM = pl.BlockSpec(memory_space=pltpu.HBM)
IN_SMEM = pl.BlockSpec(memory_space=pltpu.SMEM)


def y_transform(blocks, place, table, targets, halves, cost):
    planes, _, rows, columns = blocks.shape
    length = planes * rows
    y_rows = length // targets
    count = targets * halves
    return pl.pallas_call(
        functools.partial(y_kernel, targets, halves),
        out_shape=[jax.ShapeDtypeStruct((2, y_rows // halves, columns), jnp.bfloat16)] * count,
        in_specs=[IN_SMEM, IN_HBM, IN_HBM],
        out_specs=[IN_HBM] * count,
        scratch_shapes=[
            pltpu.VMEM((planes, 2, rows, columns), jnp.bfloat16),
            pltpu.VMEM(table.shape, jnp.bfloat16),
            pltpu.VMEM((length, 2 * columns), jnp.bfloat16),
            pltpu.VMEM((targets, 2, y_rows, columns), jnp.bfloat16),
            pltpu.SemaphoreType.DMA((targets // 2 + 1,)),
            pltpu.SemaphoreType.DMA((count,)),
        ],
        compiler_params=pltpu.CompilerParams(vmem_limit_bytes=VMEM_LIMIT),
        cost_estimate=cost,
        name="y_transform",
    )(place, blocks, table)


def z_kernel(layout, targets, component, first_row, place_ref, *refs):
    pieces, table_hbm = refs[: len(layout)], refs[len(layout)]
    field, joined, split, table, out, sems, table_sems, out_sems = refs[-8:]
    rows = joined.shape[0] // 2
    tiles, length, tile = table.shape[0], table.shape[1], table.shape[2] // 2
    columns = length // targets
    factor = 1.0 / math.sqrt(length)

    def place_piece(number):
        piece, (behind, row, lane) = pieces[number], layout[number]
        source = lax.rem(place_ref[1] + targets - behind, targets)
        _, some_rows, some_columns = piece.shape
        start = pl.multiple_of(source * columns, columns) + lane
        return [
            pltpu.make_async_copy(
                piece.at[part],
                joined.at[pl.ds(part * rows + row, some_rows), pl.ds(start, some_columns)],
                sems.at[number, part],
            )
            for part in range(2)
        ]

    loads = [copy for number in range(len(layout)) for copy in place_piece(number)]
    for copy in loads:
        copy.start()
    tables = [pltpu.make_async_copy(table_hbm.at[step], table.at[step], table_sems.at[step]) for step in range(tiles)]
    for copy in tables:
        copy.start()

    lane = lax.broadcasted_iota(jnp.int32, (columns, columns), 1)
    wanted = jnp.where(lane < columns // 2, 2 * lane, 2 * lane - (columns - 1))
    pick = jnp.where(lax.broadcasted_iota(jnp.int32, (columns, columns), 0) == wanted, 1.0, 0.0).astype(jnp.bfloat16)
    for copy in loads:
        copy.wait()
    for source in range(targets):
        parted = dot(joined[:, pl.ds(source * columns, columns)], pick).astype(jnp.bfloat16)
        split[:, pl.ds(source * columns // 2, columns // 2)] = parted[:, : columns // 2]
        split[:, pl.ds((length + source * columns) // 2, columns // 2)] = parted[:, columns // 2 :]

    def product(step, start):
        lanes = pl.ds(start, length // 2)
        both = dot(split[:, lanes], table[step, lanes, :])
        return both[:rows, :tile] - both[rows:, tile:], both[:rows, tile:] + both[rows:, :tile]

    stores = []
    for step in range(tiles):
        tables[step].wait()
        even = product(step, 0)
        odd = product(step, length // 2)
        for part in range(2):
            out[step, part] = ((even[part] + odd[part]) * factor).astype(jnp.bfloat16)
            out[step + tiles, part] = ((even[part] - odd[part]) * factor).astype(jnp.bfloat16)
        for number in (step, step + tiles):
            stores.append(
                pltpu.make_async_copy(
                    out.at[number],
                    field.at[component, :, 0, pl.ds(first_row, rows), pl.ds(number * tile, tile)],
                    out_sems.at[number],
                )
            )
            stores[-1].start()
    for copy in stores:
        copy.wait()


def z_transform(pieces, layout, place, table, targets, component, first_row, field, shape, cost):
    rows = max(row + piece.shape[1] for piece, (_, row, _) in zip(pieces, layout))
    tiles, length, _ = table.shape
    through = [] if field is None else [field]
    return pl.pallas_call(
        functools.partial(z_kernel, layout, targets, component, first_row),
        out_shape=jax.ShapeDtypeStruct(shape, jnp.bfloat16),
        in_specs=[IN_SMEM] + [IN_HBM] * (len(pieces) + 1 + len(through)),
        out_specs=IN_HBM,
        scratch_shapes=[
            pltpu.VMEM((2 * rows, length), jnp.bfloat16),
            pltpu.VMEM((2 * rows, length), jnp.bfloat16),
            pltpu.VMEM(table.shape, jnp.bfloat16),
            pltpu.VMEM((2 * tiles, 2, rows, length // tiles // 2), jnp.bfloat16),
            pltpu.SemaphoreType.DMA((len(pieces), 2)),
            pltpu.SemaphoreType.DMA((tiles,)),
            pltpu.SemaphoreType.DMA((2 * tiles,)),
        ],
        input_output_aliases={} if field is None else {len(pieces) + 2: 0},
        compiler_params=pltpu.CompilerParams(vmem_limit_bytes=VMEM_LIMIT),
        cost_estimate=cost,
        name="z_transform",
    )(place, *pieces, table, *through)


def roll_kernel(numbers, place_ref, *refs):
    slots = refs[: len(numbers)]
    out_hbm, blocks, out, sems, out_sem = refs[len(numbers) :]
    loads = [
        pltpu.make_async_copy(slot.at[:, number], blocks.at[part], sems.at[part])
        for part, (slot, number) in enumerate(zip(slots, numbers))
    ]
    for copy in loads:
        copy.start()
    for copy in loads:
        copy.wait()

    def store(block, part, values):
        out[block, part] = values

    shift_rows([blocks.at[part] for part in range(len(numbers))], place_ref[0], store, parity=False)
    copy = pltpu.make_async_copy(out, out_hbm, out_sem.at[0])
    copy.start()
    copy.wait()


def roll_planes(place, *slots):
    count, _, rows, columns = slots[0][0].shape
    return pl.pallas_call(
        functools.partial(roll_kernel, [number for _, number in slots]),
        out_shape=jax.ShapeDtypeStruct((count, len(slots), rows, columns), jnp.bfloat16),
        in_specs=[IN_SMEM] + [IN_HBM] * len(slots),
        out_specs=IN_HBM,
        scratch_shapes=[
            pltpu.VMEM((len(slots), count, rows, columns), jnp.bfloat16),
            pltpu.VMEM((count, len(slots), rows, columns), jnp.bfloat16),
            pltpu.SemaphoreType.DMA((len(slots),)),
            pltpu.SemaphoreType.DMA((1,)),
        ],
        compiler_params=pltpu.CompilerParams(vmem_limit_bytes=VMEM_LIMIT),
        cost_estimate=COST,
        name="roll_planes",
    )(place, *[blocks for blocks, _ in slots])


def restack_kernel(steps, from_hbm, out_hbm, held, sems, out_sems):
    loads = [pltpu.make_async_copy(from_hbm.at[source], held.at[part], sems.at[part]) for part, (source, _) in enumerate(steps)]
    for copy in loads:
        copy.start()
    stores = []
    for part, (_, target) in enumerate(steps):
        loads[part].wait()
        stores.append(pltpu.make_async_copy(held.at[part], out_hbm.at[target], out_sems.at[part]))
        stores[-1].start()
    for copy in stores:
        copy.wait()


def restack(array, steps, part, shape, name):
    return pl.pallas_call(
        functools.partial(restack_kernel, steps),
        out_shape=jax.ShapeDtypeStruct(shape, array.dtype),
        in_specs=[IN_HBM],
        out_specs=IN_HBM,
        scratch_shapes=[
            pltpu.VMEM((len(steps), *part), array.dtype),
            pltpu.SemaphoreType.DMA((len(steps),)),
            pltpu.SemaphoreType.DMA((len(steps),)),
        ],
        compiler_params=pltpu.CompilerParams(vmem_limit_bytes=VMEM_LIMIT),
        cost_estimate=COST,
        name=name,
    )(array)


def by_plane(fields, *slots, lanes=None):
    _, _, planes, rows, columns = fields.shape
    start, stop = lanes or (0, columns)
    steps = [
        ((*slot, slice(None), slice(None), pl.ds(start, stop - start)), (slice(None), number))
        for number, slot in enumerate(slots)
    ]
    part = (planes, rows, stop - start)
    return restack(fields, steps, part, (planes, len(slots), rows, stop - start), "by_plane")


def by_part(planes):
    count, parts, rows, columns = planes.shape
    steps = [((slice(None), part), (part,)) for part in range(parts)]
    return restack(planes, steps, (count, rows, columns), (parts, count, rows, columns), "by_part")


def nothing_kernel(*refs):
    pass


def after(array, *others, cost=COST):
    anywhere = IN_HBM
    return pl.pallas_call(
        nothing_kernel,
        out_shape=jax.ShapeDtypeStruct(array.shape, array.dtype),
        in_specs=[anywhere] * (1 + len(others)),
        out_specs=anywhere,
        input_output_aliases={0: 0},
        compiler_params=pltpu.CompilerParams(vmem_limit_bytes=VMEM_LIMIT),
        cost_estimate=cost,
        name="after",
    )(array, *others)


def exchange(blocks):
    return lax.all_to_all(blocks, "ky", 0, 0, tiled=True)


def along_z(others):
    targets = len(others) + 1
    return [
        lax.ppermute(piece, "kz", [(i, (i + step) % targets) for i in range(targets)])
        for step, piece in enumerate(others, 1)
    ]


def shards(fields, offsets):
    components = fields.shape[0] - 1
    targets = lax.axis_size("kz")
    assert fields.shape[2] == lax.axis_size("ky") and components == 3
    place = jnp.stack([offsets[lax.axis_index("ky")], lax.axis_index("kz").astype(jnp.int32)])
    y_rows = fields.shape[3] * lax.axis_size("ky") // targets
    shape = (components, 2, 1, y_rows, fields.shape[4] * targets)
    ky_table = y_table(y_rows * targets, targets)
    kz_table = z_table(shape[-1], 256)

    def y_of(blocks, halves, cost=COST):
        pieces = y_transform(blocks, place, ky_table, targets, halves, cost)
        groups = [pieces[half * targets : (half + 1) * targets] for half in range(halves)]
        return [[group[0], *along_z(group[1:])] for group in groups]

    def z_of(groups, starts, component, first_row, field, cost=COST):
        layout = [(behind, *start) for start in starts for behind in range(targets)]
        pieces = [piece for group in groups for piece in group]
        return z_transform(pieces, layout, place, kz_table, targets, component, first_row, field, shape, cost)

    by_rows = [(0, 0), (y_rows // 2, 0)]
    fields0 = by_plane(fields, (0, 0), (0, 1))
    fields1 = by_plane(fields, (1, 0), (1, 1))
    fields2 = by_plane(fields, (2, 0), (2, 1), (components, 0), (components, 1))
    blocks0 = exchange(fields0)
    (pieces0,) = y_of(blocks0, 1, HIGH)
    blocks1 = exchange(fields1)
    (pieces1,) = y_of(blocks1, 1, MID)
    blocks2 = exchange(fields2)
    field = z_of([pieces0], by_rows[:1], 0, 0, None, HIGH)
    blocks2 = after(blocks2, field)
    (pieces2,) = y_of(blocks2, 1)
    plane = roll_planes(place, (blocks2, 2), (blocks2, 3))
    scalar = by_part(exchange(plane))
    field = z_of([pieces1], by_rows[:1], 1, 0, field)
    field = z_of([pieces2], by_rows[:1], 2, 0, field, HIGH)
    return (field, scalar)


def solution(mesh):
    placed = (P(None, None, None, "ky", "kz"), P())
    return jax.shard_map(
        shards,
        mesh=mesh,
        in_specs=placed,
        out_specs=(P(None, None, "ky", "kz", None), P(None, None, "ky", "kz")),
        check_vma=False,
    )
```

```python
import functools
import math

import jax
import jax.numpy as jnp
import ml_dtypes
import numpy as np
from jax import lax
from jax.experimental import pallas as pl
from jax.experimental.pallas import tpu as pltpu
from jax.sharding import PartitionSpec as P

VMEM_LIMIT = 64 * 1024 * 1024
COST = pl.CostEstimate(flops=0, bytes_accessed=0, transcendentals=0)
MID = pl.CostEstimate(flops=8_000_000_000, bytes_accessed=0, transcendentals=0)
HIGH = pl.CostEstimate(flops=40_000_000_000, bytes_accessed=0, transcendentals=0)


def tables(length):
    counter = np.arange(length, dtype=np.int64)
    product = (counter[:, None] * counter[None, :]) % length
    angles = product.astype(np.float32) * np.float32(2.0 * math.pi / length)
    return (np.cos(angles).astype(ml_dtypes.bfloat16), np.sin(angles).astype(ml_dtypes.bfloat16))


def y_table(length, targets):
    order = np.concatenate([np.arange(0, length, 2), np.arange(1, length, 2)])
    parts = [table[: length // 2, order].reshape(targets // 2, length // targets, length) for table in tables(length)]
    return jnp.asarray(np.concatenate(parts, axis=1))


def z_table(length, tile):
    half = length // 2
    order = np.concatenate([np.arange(0, length, 2), np.arange(1, length, 2)])
    parts = [table[order, :half].reshape(length, half // tile, tile).swapaxes(0, 1) for table in tables(length)]
    return jnp.asarray(np.concatenate(parts, axis=2))


def dot(left, right):
    return lax.dot_general(left, right, (((1,), (0,)), ((), ())), preferred_element_type=jnp.float32)


def shift_rows(slots, offset, store, parity, scale=1.0):
    count, rows, _ = slots[0].shape
    whole, rest = offset // rows, offset % rows
    to_row = lax.broadcasted_iota(jnp.int32, (rows, 2 * rows), 0)
    if parity:
        to_row = jnp.where(to_row < rows // 2, 2 * to_row, 2 * to_row - (rows - 1))
    from_row = lax.broadcasted_iota(jnp.int32, (rows, 2 * rows), 1)
    pick = jnp.where(from_row == rows + to_row - rest, scale, 0.0).astype(jnp.bfloat16)
    for block in range(count):
        here = lax.rem(block - whole + count, count)
        before = lax.rem(block - whole - 1 + 2 * count, count)
        for part, slot in enumerate(slots):
            window = jnp.concatenate([slot[before], slot[here]], axis=0)
            store(block, part, dot(pick, window).astype(jnp.bfloat16))


def y_kernel(targets, halves, place_ref, blocks_hbm, table_hbm, *refs):
    count = targets * halves
    outs, (blocks, table, rolled, pieces, sems, out_sems) = refs[:count], refs[count:]
    planes, _, rows, columns = blocks.shape
    length = planes * rows
    y_rows = length // targets
    half_rows = y_rows // halves
    pairs = targets // 2
    factor = 1.0 / math.sqrt(length)
    assert math.frexp(factor)[0] == 0.5

    load = pltpu.make_async_copy(blocks_hbm.at[:, pl.ds(0, 2)], blocks, sems.at[pairs])
    load.start()
    loads = []
    for step in range(pairs):
        wanted = lax.rem(place_ref[1] + step, pairs)
        loads.append(pltpu.make_async_copy(table_hbm.at[wanted], table.at[step], sems.at[step]))
        loads[-1].start()
    load.wait()

    def store(block, part, values):
        lanes = pl.ds(part * columns, columns)
        for odd in range(2):
            start = odd * (length // 2) + block * (rows // 2)
            rolled[pl.ds(start, rows // 2), lanes] = values[odd * (rows // 2) : (odd + 1) * (rows // 2)]

    shift_rows([blocks.at[:, part] for part in range(2)], place_ref[0], store, parity=True, scale=factor)

    def product(step, start):
        both = dot(table[step, :, pl.ds(start, length // 2)], rolled[pl.ds(start, length // 2), :])
        real = both[:y_rows, :columns] - both[y_rows:, columns:]
        imag = both[y_rows:, :columns] + both[:y_rows, columns:]
        return real, imag

    stores = []
    for step in range(pairs):
        loads[step].wait()
        sign = jnp.where(lax.rem(place_ref[1] + step, targets) < pairs, 1.0, -1.0)
        even = product(step, 0)
        odd = product(step, length // 2)
        for part in range(2):
            from_even, from_odd = even[part], odd[part] * sign
            pieces[step, part] = (from_even + from_odd).astype(jnp.bfloat16)
            pieces[step + pairs, part] = (from_even - from_odd).astype(jnp.bfloat16)
        for index in (step, step + pairs):
            for half in range(halves):
                number = half * targets + index
                stores.append(
                    pltpu.make_async_copy(
                        pieces.at[index, :, pl.ds(half * half_rows, half_rows)], outs[number], out_sems.at[number]
                    )
                )
                stores[-1].start()
    for copy in stores:
        copy.wait()


IN_HBM = pl.BlockSpec(memory_space=pltpu.HBM)
IN_SMEM = pl.BlockSpec(memory_space=pltpu.SMEM)


def y_transform(blocks, place, table, targets, halves, cost):
    planes, _, rows, columns = blocks.shape
    length = planes * rows
    y_rows = length // targets
    count = targets * halves
    return pl.pallas_call(
        functools.partial(y_kernel, targets, halves),
        out_shape=[jax.ShapeDtypeStruct((2, y_rows // halves, columns), jnp.bfloat16)] * count,
        in_specs=[IN_SMEM, IN_HBM, IN_HBM],
        out_specs=[IN_HBM] * count,
        scratch_shapes=[
            pltpu.VMEM((planes, 2, rows, columns), jnp.bfloat16),
            pltpu.VMEM(table.shape, jnp.bfloat16),
            pltpu.VMEM((length, 2 * columns), jnp.bfloat16),
            pltpu.VMEM((targets, 2, y_rows, columns), jnp.bfloat16),
            pltpu.SemaphoreType.DMA((targets // 2 + 1,)),
            pltpu.SemaphoreType.DMA((count,)),
        ],
        compiler_params=pltpu.CompilerParams(vmem_limit_bytes=VMEM_LIMIT),
        cost_estimate=cost,
        name="y_transform",
    )(place, blocks, table)


def z_kernel(layout, targets, component, first_row, place_ref, *refs):
    pieces, table_hbm = refs[: len(layout)], refs[len(layout)]
    field, joined, split, table, out, sems, table_sems, out_sems = refs[-8:]
    rows = joined.shape[0] // 2
    tiles, length, tile = table.shape[0], table.shape[1], table.shape[2] // 2
    columns = length // targets
    factor = 1.0 / math.sqrt(length)
    assert math.frexp(factor)[0] == 0.5

    def place_piece(number):
        piece, (behind, row, lane) = pieces[number], layout[number]
        source = lax.rem(place_ref[1] + targets - behind, targets)
        _, some_rows, some_columns = piece.shape
        start = pl.multiple_of(source * columns, columns) + lane
        return [
            pltpu.make_async_copy(
                piece.at[part],
                joined.at[pl.ds(part * rows + row, some_rows), pl.ds(start, some_columns)],
                sems.at[number, part],
            )
            for part in range(2)
        ]

    loads = [copy for number in range(len(layout)) for copy in place_piece(number)]
    for copy in loads:
        copy.start()
    tables = [pltpu.make_async_copy(table_hbm.at[step], table.at[step], table_sems.at[step]) for step in range(tiles)]
    for copy in tables:
        copy.start()

    lane = lax.broadcasted_iota(jnp.int32, (columns, columns), 1)
    wanted = jnp.where(lane < columns // 2, 2 * lane, 2 * lane - (columns - 1))
    pick = jnp.where(lax.broadcasted_iota(jnp.int32, (columns, columns), 0) == wanted, factor, 0.0).astype(jnp.bfloat16)
    for copy in loads:
        copy.wait()
    for source in range(targets):
        parted = dot(joined[:, pl.ds(source * columns, columns)], pick).astype(jnp.bfloat16)
        split[:, pl.ds(source * columns // 2, columns // 2)] = parted[:, : columns // 2]
        split[:, pl.ds((length + source * columns) // 2, columns // 2)] = parted[:, columns // 2 :]

    def product(step, start):
        lanes = pl.ds(start, length // 2)
        both = dot(split[:, lanes], table[step, lanes, :])
        return both[:rows, :tile] - both[rows:, tile:], both[:rows, tile:] + both[rows:, :tile]

    stores = []
    for step in range(tiles):
        tables[step].wait()
        even = product(step, 0)
        odd = product(step, length // 2)
        for part in range(2):
            out[step, part] = (even[part] + odd[part]).astype(jnp.bfloat16)
            out[step + tiles, part] = (even[part] - odd[part]).astype(jnp.bfloat16)
        for number in (step, step + tiles):
            stores.append(
                pltpu.make_async_copy(
                    out.at[number],
                    field.at[component, :, 0, pl.ds(first_row, rows), pl.ds(number * tile, tile)],
                    out_sems.at[number],
                )
            )
            stores[-1].start()
    for copy in stores:
        copy.wait()


def z_transform(pieces, layout, place, table, targets, component, first_row, field, shape, cost):
    rows = max(row + piece.shape[1] for piece, (_, row, _) in zip(pieces, layout))
    tiles, length, _ = table.shape
    through = [] if field is None else [field]
    return pl.pallas_call(
        functools.partial(z_kernel, layout, targets, component, first_row),
        out_shape=jax.ShapeDtypeStruct(shape, jnp.bfloat16),
        in_specs=[IN_SMEM] + [IN_HBM] * (len(pieces) + 1 + len(through)),
        out_specs=IN_HBM,
        scratch_shapes=[
            pltpu.VMEM((2 * rows, length), jnp.bfloat16),
            pltpu.VMEM((2 * rows, length), jnp.bfloat16),
            pltpu.VMEM(table.shape, jnp.bfloat16),
            pltpu.VMEM((2 * tiles, 2, rows, length // tiles // 2), jnp.bfloat16),
            pltpu.SemaphoreType.DMA((len(pieces), 2)),
            pltpu.SemaphoreType.DMA((tiles,)),
            pltpu.SemaphoreType.DMA((2 * tiles,)),
        ],
        input_output_aliases={} if field is None else {len(pieces) + 2: 0},
        compiler_params=pltpu.CompilerParams(vmem_limit_bytes=VMEM_LIMIT),
        cost_estimate=cost,
        name="z_transform",
    )(place, *pieces, table, *through)


def roll_kernel(numbers, place_ref, *refs):
    slots = refs[: len(numbers)]
    out_hbm, blocks, out, sems, out_sem = refs[len(numbers) :]
    loads = [
        pltpu.make_async_copy(slot.at[:, number], blocks.at[part], sems.at[part])
        for part, (slot, number) in enumerate(zip(slots, numbers))
    ]
    for copy in loads:
        copy.start()
    for copy in loads:
        copy.wait()

    def store(block, part, values):
        out[block, part] = values

    shift_rows([blocks.at[part] for part in range(len(numbers))], place_ref[0], store, parity=False)
    copy = pltpu.make_async_copy(out, out_hbm, out_sem.at[0])
    copy.start()
    copy.wait()


def roll_planes(place, *slots):
    count, _, rows, columns = slots[0][0].shape
    return pl.pallas_call(
        functools.partial(roll_kernel, [number for _, number in slots]),
        out_shape=jax.ShapeDtypeStruct((count, len(slots), rows, columns), jnp.bfloat16),
        in_specs=[IN_SMEM] + [IN_HBM] * len(slots),
        out_specs=IN_HBM,
        scratch_shapes=[
            pltpu.VMEM((len(slots), count, rows, columns), jnp.bfloat16),
            pltpu.VMEM((count, len(slots), rows, columns), jnp.bfloat16),
            pltpu.SemaphoreType.DMA((len(slots),)),
            pltpu.SemaphoreType.DMA((1,)),
        ],
        compiler_params=pltpu.CompilerParams(vmem_limit_bytes=VMEM_LIMIT),
        cost_estimate=COST,
        name="roll_planes",
    )(place, *[blocks for blocks, _ in slots])


def restack_kernel(steps, from_hbm, out_hbm, held, sems, out_sems):
    loads = [pltpu.make_async_copy(from_hbm.at[source], held.at[part], sems.at[part]) for part, (source, _) in enumerate(steps)]
    for copy in loads:
        copy.start()
    stores = []
    for part, (_, target) in enumerate(steps):
        loads[part].wait()
        stores.append(pltpu.make_async_copy(held.at[part], out_hbm.at[target], out_sems.at[part]))
        stores[-1].start()
    for copy in stores:
        copy.wait()


def restack(array, steps, part, shape, name):
    return pl.pallas_call(
        functools.partial(restack_kernel, steps),
        out_shape=jax.ShapeDtypeStruct(shape, array.dtype),
        in_specs=[IN_HBM],
        out_specs=IN_HBM,
        scratch_shapes=[
            pltpu.VMEM((len(steps), *part), array.dtype),
            pltpu.SemaphoreType.DMA((len(steps),)),
            pltpu.SemaphoreType.DMA((len(steps),)),
        ],
        compiler_params=pltpu.CompilerParams(vmem_limit_bytes=VMEM_LIMIT),
        cost_estimate=COST,
        name=name,
    )(array)


def by_plane(fields, *slots, lanes=None):
    _, _, planes, rows, columns = fields.shape
    start, stop = lanes or (0, columns)
    steps = [
        ((*slot, slice(None), slice(None), pl.ds(start, stop - start)), (slice(None), number))
        for number, slot in enumerate(slots)
    ]
    part = (planes, rows, stop - start)
    return restack(fields, steps, part, (planes, len(slots), rows, stop - start), "by_plane")


def by_part(planes):
    count, parts, rows, columns = planes.shape
    steps = [((slice(None), part), (part,)) for part in range(parts)]
    return restack(planes, steps, (count, rows, columns), (parts, count, rows, columns), "by_part")


def nothing_kernel(*refs):
    pass


def after(array, *others, cost=COST):
    anywhere = IN_HBM
    return pl.pallas_call(
        nothing_kernel,
        out_shape=jax.ShapeDtypeStruct(array.shape, array.dtype),
        in_specs=[anywhere] * (1 + len(others)),
        out_specs=anywhere,
        input_output_aliases={0: 0},
        compiler_params=pltpu.CompilerParams(vmem_limit_bytes=VMEM_LIMIT),
        cost_estimate=cost,
        name="after",
    )(array, *others)


def exchange(blocks):
    return lax.all_to_all(blocks, "ky", 0, 0, tiled=True)


def along_z(others):
    targets = len(others) + 1
    return [
        lax.ppermute(piece, "kz", [(i, (i + step) % targets) for i in range(targets)])
        for step, piece in enumerate(others, 1)
    ]


def shards(fields, offsets):
    components = fields.shape[0] - 1
    targets = lax.axis_size("kz")
    assert fields.shape[2] == lax.axis_size("ky") and components == 3
    place = jnp.stack([offsets[lax.axis_index("ky")], lax.axis_index("kz").astype(jnp.int32)])
    y_rows = fields.shape[3] * lax.axis_size("ky") // targets
    shape = (components, 2, 1, y_rows, fields.shape[4] * targets)
    ky_table = y_table(y_rows * targets, targets)
    kz_table = z_table(shape[-1], 256)

    def y_of(blocks, halves, cost=COST):
        pieces = y_transform(blocks, place, ky_table, targets, halves, cost)
        groups = [pieces[half * targets : (half + 1) * targets] for half in range(halves)]
        return [[group[0], *along_z(group[1:])] for group in groups]

    def z_of(groups, starts, component, first_row, field, cost=COST):
        layout = [(behind, *start) for start in starts for behind in range(targets)]
        pieces = [piece for group in groups for piece in group]
        return z_transform(pieces, layout, place, kz_table, targets, component, first_row, field, shape, cost)

    by_rows = [(0, 0), (y_rows // 2, 0)]
    fields0 = by_plane(fields, (0, 0), (0, 1))
    fields1 = by_plane(fields, (1, 0), (1, 1))
    fields2 = by_plane(fields, (2, 0), (2, 1), (components, 0), (components, 1))
    blocks0 = exchange(fields0)
    (pieces0,) = y_of(blocks0, 1, HIGH)
    blocks1 = exchange(fields1)
    (pieces1,) = y_of(blocks1, 1, MID)
    blocks2 = exchange(fields2)
    field = z_of([pieces0], by_rows[:1], 0, 0, None, HIGH)
    blocks2 = after(blocks2, field)
    (pieces2,) = y_of(blocks2, 1)
    plane = roll_planes(place, (blocks2, 2), (blocks2, 3))
    scalar = by_part(exchange(plane))
    field = z_of([pieces1], by_rows[:1], 1, 0, field)
    field = z_of([pieces2], by_rows[:1], 2, 0, field, HIGH)
    return (field, scalar)


def solution(mesh):
    placed = (P(None, None, None, "ky", "kz"), P())
    return jax.shard_map(
        shards,
        mesh=mesh,
        in_specs=placed,
        out_specs=(P(None, None, "ky", "kz", None), P(None, None, "ky", "kz")),
        check_vma=False,
    )
```

```python
import functools
import math

import jax
import jax.numpy as jnp
import ml_dtypes
import numpy as np
from jax import lax
from jax.experimental import pallas as pl
from jax.experimental.pallas import tpu as pltpu
from jax.sharding import PartitionSpec as P

VMEM_LIMIT = 64 * 1024 * 1024
COST = pl.CostEstimate(flops=0, bytes_accessed=0, transcendentals=0)
MID = pl.CostEstimate(flops=8_000_000_000, bytes_accessed=0, transcendentals=0)
HIGH = pl.CostEstimate(flops=40_000_000_000, bytes_accessed=0, transcendentals=0)


def tables(length):
    counter = np.arange(length, dtype=np.int64)
    product = (counter[:, None] * counter[None, :]) % length
    angles = product.astype(np.float32) * np.float32(2.0 * math.pi / length)
    return (np.cos(angles).astype(ml_dtypes.bfloat16), np.sin(angles).astype(ml_dtypes.bfloat16))


def y_table(length, targets):
    order = np.concatenate([np.arange(0, length, 2), np.arange(1, length, 2)])
    parts = [table[: length // 2, order].reshape(targets // 2, length // targets, length) for table in tables(length)]
    return jnp.asarray(np.concatenate(parts, axis=1))


def z_table(length, tile):
    half = length // 2
    order = np.concatenate([np.arange(0, length, 2), np.arange(1, length, 2)])
    parts = [table[order, :half].reshape(length, half // tile, tile).swapaxes(0, 1) for table in tables(length)]
    return jnp.asarray(np.concatenate(parts, axis=2))


def dot(left, right):
    return lax.dot_general(left, right, (((1,), (0,)), ((), ())), preferred_element_type=jnp.float32)


def shift_rows(slots, offset, store, parity, scale=1.0):
    count, rows, _ = slots[0].shape
    whole, rest = offset // rows, offset % rows
    to_row = lax.broadcasted_iota(jnp.int32, (rows, 2 * rows), 0)
    if parity:
        to_row = jnp.where(to_row < rows // 2, 2 * to_row, 2 * to_row - (rows - 1))
    from_row = lax.broadcasted_iota(jnp.int32, (rows, 2 * rows), 1)
    pick = jnp.where(from_row == rows + to_row - rest, scale, 0.0).astype(jnp.bfloat16)
    for block in range(count):
        here = lax.rem(block - whole + count, count)
        before = lax.rem(block - whole - 1 + 2 * count, count)
        for part, slot in enumerate(slots):
            window = jnp.concatenate([slot[before], slot[here]], axis=0)
            store(block, part, dot(pick, window).astype(jnp.bfloat16))


def y_kernel(targets, halves, place_ref, blocks_hbm, table_hbm, *refs):
    count = targets * halves
    outs, (blocks, table, rolled, pieces, sems, out_sems) = refs[:count], refs[count:]
    planes, _, rows, columns = blocks.shape
    length = planes * rows
    y_rows = length // targets
    half_rows = y_rows // halves
    pairs = targets // 2
    factor = 1.0 / math.sqrt(length)
    assert math.frexp(factor)[0] == 0.5

    load = pltpu.make_async_copy(blocks_hbm.at[:, pl.ds(0, 2)], blocks, sems.at[pairs])
    load.start()
    loads = []
    for step in range(pairs):
        wanted = lax.rem(place_ref[1] + step, pairs)
        loads.append(pltpu.make_async_copy(table_hbm.at[wanted], table.at[step], sems.at[step]))
        loads[-1].start()
    load.wait()

    def store(block, part, values):
        lanes = pl.ds(part * columns, columns)
        for odd in range(2):
            start = odd * (length // 2) + block * (rows // 2)
            rolled[pl.ds(start, rows // 2), lanes] = values[odd * (rows // 2) : (odd + 1) * (rows // 2)]

    shift_rows([blocks.at[:, part] for part in range(2)], place_ref[0], store, parity=True, scale=factor)

    def product(step, start):
        both = dot(table[step, :, pl.ds(start, length // 2)], rolled[pl.ds(start, length // 2), :])
        real = both[:y_rows, :columns] - both[y_rows:, columns:]
        imag = both[y_rows:, :columns] + both[:y_rows, columns:]
        return real, imag

    stores = []
    for step in range(pairs):
        loads[step].wait()
        sign = jnp.where(lax.rem(place_ref[1] + step, targets) < pairs, 1.0, -1.0)
        even = product(step, 0)
        odd = product(step, length // 2)
        for part in range(2):
            from_even, from_odd = even[part], odd[part] * sign
            pieces[step, part] = (from_even + from_odd).astype(jnp.bfloat16)
            pieces[step + pairs, part] = (from_even - from_odd).astype(jnp.bfloat16)
        for index in (step, step + pairs):
            for half in range(halves):
                number = half * targets + index
                stores.append(
                    pltpu.make_async_copy(
                        pieces.at[index, :, pl.ds(half * half_rows, half_rows)], outs[number], out_sems.at[number]
                    )
                )
                stores[-1].start()
    for copy in stores:
        copy.wait()


IN_HBM = pl.BlockSpec(memory_space=pltpu.HBM)
IN_SMEM = pl.BlockSpec(memory_space=pltpu.SMEM)


def y_transform(blocks, place, table, targets, halves, cost):
    planes, _, rows, columns = blocks.shape
    length = planes * rows
    y_rows = length // targets
    count = targets * halves
    return pl.pallas_call(
        functools.partial(y_kernel, targets, halves),
        out_shape=[jax.ShapeDtypeStruct((2, y_rows // halves, columns), jnp.bfloat16)] * count,
        in_specs=[IN_SMEM, IN_HBM, IN_HBM],
        out_specs=[IN_HBM] * count,
        scratch_shapes=[
            pltpu.VMEM((planes, 2, rows, columns), jnp.bfloat16),
            pltpu.VMEM(table.shape, jnp.bfloat16),
            pltpu.VMEM((length, 2 * columns), jnp.bfloat16),
            pltpu.VMEM((targets, 2, y_rows, columns), jnp.bfloat16),
            pltpu.SemaphoreType.DMA((targets // 2 + 1,)),
            pltpu.SemaphoreType.DMA((count,)),
        ],
        compiler_params=pltpu.CompilerParams(vmem_limit_bytes=VMEM_LIMIT),
        cost_estimate=cost,
        name="y_transform",
    )(place, blocks, table)


def z_kernel(layout, targets, component, first_row, place_ref, *refs):
    pieces, table_hbm = refs[: len(layout)], refs[len(layout)]
    field, joined, split, table, out, sems, table_sems, out_sems = refs[-8:]
    rows = joined.shape[0] // 2
    tiles, length, tile = table.shape[0], table.shape[1], table.shape[2] // 2
    columns = length // targets
    factor = 1.0 / math.sqrt(length)
    assert math.frexp(factor)[0] == 0.5

    def place_piece(number):
        piece, (behind, row, lane) = pieces[number], layout[number]
        source = lax.rem(place_ref[1] + targets - behind, targets)
        _, some_rows, some_columns = piece.shape
        start = pl.multiple_of(source * columns, columns) + lane
        return [
            pltpu.make_async_copy(
                piece.at[part],
                joined.at[pl.ds(part * rows + row, some_rows), pl.ds(start, some_columns)],
                sems.at[number, part],
            )
            for part in range(2)
        ]

    loads = [copy for number in range(len(layout)) for copy in place_piece(number)]
    for copy in loads:
        copy.start()
    tables = [pltpu.make_async_copy(table_hbm.at[step], table.at[step], table_sems.at[step]) for step in range(tiles)]
    for copy in tables:
        copy.start()

    lane = lax.broadcasted_iota(jnp.int32, (columns, columns), 1)
    wanted = jnp.where(lane < columns // 2, 2 * lane, 2 * lane - (columns - 1))
    pick = jnp.where(lax.broadcasted_iota(jnp.int32, (columns, columns), 0) == wanted, factor, 0.0).astype(jnp.bfloat16)
    for copy in loads:
        copy.wait()
    for source in range(targets):
        parted = dot(joined[:, pl.ds(source * columns, columns)], pick).astype(jnp.bfloat16)
        split[:, pl.ds(source * columns // 2, columns // 2)] = parted[:, : columns // 2]
        split[:, pl.ds((length + source * columns) // 2, columns // 2)] = parted[:, columns // 2 :]

    def product(step, start):
        lanes = pl.ds(start, length // 2)
        both = dot(split[:, lanes], table[step, lanes, :])
        return both[:rows, :tile] - both[rows:, tile:], both[:rows, tile:] + both[rows:, :tile]

    stores = []
    for step in range(tiles):
        tables[step].wait()
        even = product(step, 0)
        odd = product(step, length // 2)
        for part in range(2):
            out[step, part] = (even[part] + odd[part]).astype(jnp.bfloat16)
            out[step + tiles, part] = (even[part] - odd[part]).astype(jnp.bfloat16)
        for number in (step, step + tiles):
            stores.append(
                pltpu.make_async_copy(
                    out.at[number],
                    field.at[component, :, 0, pl.ds(first_row, rows), pl.ds(number * tile, tile)],
                    out_sems.at[number],
                )
            )
            stores[-1].start()
    for copy in stores:
        copy.wait()


def z_transform(pieces, layout, place, table, targets, component, first_row, field, shape, cost):
    rows = max(row + piece.shape[1] for piece, (_, row, _) in zip(pieces, layout))
    tiles, length, _ = table.shape
    through = [] if field is None else [field]
    return pl.pallas_call(
        functools.partial(z_kernel, layout, targets, component, first_row),
        out_shape=jax.ShapeDtypeStruct(shape, jnp.bfloat16),
        in_specs=[IN_SMEM] + [IN_HBM] * (len(pieces) + 1 + len(through)),
        out_specs=IN_HBM,
        scratch_shapes=[
            pltpu.VMEM((2 * rows, length), jnp.bfloat16),
            pltpu.VMEM((2 * rows, length), jnp.bfloat16),
            pltpu.VMEM(table.shape, jnp.bfloat16),
            pltpu.VMEM((2 * tiles, 2, rows, length // tiles // 2), jnp.bfloat16),
            pltpu.SemaphoreType.DMA((len(pieces), 2)),
            pltpu.SemaphoreType.DMA((tiles,)),
            pltpu.SemaphoreType.DMA((2 * tiles,)),
        ],
        input_output_aliases={} if field is None else {len(pieces) + 2: 0},
        compiler_params=pltpu.CompilerParams(vmem_limit_bytes=VMEM_LIMIT // 4 if field is not None else VMEM_LIMIT),
        cost_estimate=cost,
        name="z_transform",
    )(place, *pieces, table, *through)


def roll_kernel(numbers, place_ref, *refs):
    slots = refs[: len(numbers)]
    out_hbm, blocks, out, sems, out_sem = refs[len(numbers) :]
    loads = [
        pltpu.make_async_copy(slot.at[:, number], blocks.at[part], sems.at[part])
        for part, (slot, number) in enumerate(zip(slots, numbers))
    ]
    for copy in loads:
        copy.start()
    for copy in loads:
        copy.wait()

    def store(block, part, values):
        out[block, part] = values

    shift_rows([blocks.at[part] for part in range(len(numbers))], place_ref[0], store, parity=False)
    copy = pltpu.make_async_copy(out, out_hbm, out_sem.at[0])
    copy.start()
    copy.wait()


def roll_planes(place, *slots):
    count, _, rows, columns = slots[0][0].shape
    return pl.pallas_call(
        functools.partial(roll_kernel, [number for _, number in slots]),
        out_shape=jax.ShapeDtypeStruct((count, len(slots), rows, columns), jnp.bfloat16),
        in_specs=[IN_SMEM] + [IN_HBM] * len(slots),
        out_specs=IN_HBM,
        scratch_shapes=[
            pltpu.VMEM((len(slots), count, rows, columns), jnp.bfloat16),
            pltpu.VMEM((count, len(slots), rows, columns), jnp.bfloat16),
            pltpu.SemaphoreType.DMA((len(slots),)),
            pltpu.SemaphoreType.DMA((1,)),
        ],
        compiler_params=pltpu.CompilerParams(vmem_limit_bytes=VMEM_LIMIT),
        cost_estimate=COST,
        name="roll_planes",
    )(place, *[blocks for blocks, _ in slots])


def restack_kernel(steps, from_hbm, out_hbm, held, sems, out_sems):
    loads = [pltpu.make_async_copy(from_hbm.at[source], held.at[part], sems.at[part]) for part, (source, _) in enumerate(steps)]
    for copy in loads:
        copy.start()
    stores = []
    for part, (_, target) in enumerate(steps):
        loads[part].wait()
        stores.append(pltpu.make_async_copy(held.at[part], out_hbm.at[target], out_sems.at[part]))
        stores[-1].start()
    for copy in stores:
        copy.wait()


def restack(array, steps, part, shape, name):
    return pl.pallas_call(
        functools.partial(restack_kernel, steps),
        out_shape=jax.ShapeDtypeStruct(shape, array.dtype),
        in_specs=[IN_HBM],
        out_specs=IN_HBM,
        scratch_shapes=[
            pltpu.VMEM((len(steps), *part), array.dtype),
            pltpu.SemaphoreType.DMA((len(steps),)),
            pltpu.SemaphoreType.DMA((len(steps),)),
        ],
        compiler_params=pltpu.CompilerParams(vmem_limit_bytes=VMEM_LIMIT if name == "by_plane" else VMEM_LIMIT // 4),
        cost_estimate=COST,
        name=name,
    )(array)


def by_plane(fields, *slots, lanes=None):
    _, _, planes, rows, columns = fields.shape
    start, stop = lanes or (0, columns)
    steps = [
        ((*slot, slice(None), slice(None), pl.ds(start, stop - start)), (slice(None), number))
        for number, slot in enumerate(slots)
    ]
    part = (planes, rows, stop - start)
    return restack(fields, steps, part, (planes, len(slots), rows, stop - start), "by_plane")


def by_part(planes):
    count, parts, rows, columns = planes.shape
    steps = [((slice(None), part), (part,)) for part in range(parts)]
    return restack(planes, steps, (count, rows, columns), (parts, count, rows, columns), "by_part")


def nothing_kernel(*refs):
    pass


def after(array, *others, cost=COST):
    anywhere = IN_HBM
    return pl.pallas_call(
        nothing_kernel,
        out_shape=jax.ShapeDtypeStruct(array.shape, array.dtype),
        in_specs=[anywhere] * (1 + len(others)),
        out_specs=anywhere,
        input_output_aliases={0: 0},
        compiler_params=pltpu.CompilerParams(vmem_limit_bytes=VMEM_LIMIT),
        cost_estimate=cost,
        name="after",
    )(array, *others)


def exchange(blocks):
    return lax.all_to_all(blocks, "ky", 0, 0, tiled=True)


def along_z(others):
    targets = len(others) + 1
    return [
        lax.ppermute(piece, "kz", [(i, (i + step) % targets) for i in range(targets)])
        for step, piece in enumerate(others, 1)
    ]


def shards(fields, offsets):
    components = fields.shape[0] - 1
    targets = lax.axis_size("kz")
    assert fields.shape[2] == lax.axis_size("ky") and components == 3
    place = jnp.stack([offsets[lax.axis_index("ky")], lax.axis_index("kz").astype(jnp.int32)])
    y_rows = fields.shape[3] * lax.axis_size("ky") // targets
    shape = (components, 2, 1, y_rows, fields.shape[4] * targets)
    ky_table = y_table(y_rows * targets, targets)
    kz_table = z_table(shape[-1], 256)

    def y_of(blocks, halves, cost=COST):
        pieces = y_transform(blocks, place, ky_table, targets, halves, cost)
        groups = [pieces[half * targets : (half + 1) * targets] for half in range(halves)]
        return [[group[0], *along_z(group[1:])] for group in groups]

    def z_of(groups, starts, component, first_row, field, cost=COST):
        layout = [(behind, *start) for start in starts for behind in range(targets)]
        pieces = [piece for group in groups for piece in group]
        return z_transform(pieces, layout, place, kz_table, targets, component, first_row, field, shape, cost)

    by_rows = [(0, 0), (y_rows // 2, 0)]
    fields0 = by_plane(fields, (0, 0), (0, 1))
    fields1 = by_plane(fields, (1, 0), (1, 1))
    fields2 = by_plane(fields, (2, 0), (2, 1), (components, 0), (components, 1))
    blocks0 = exchange(fields0)
    (pieces0,) = y_of(blocks0, 1, HIGH)
    blocks1 = exchange(fields1)
    (pieces1,) = y_of(blocks1, 1, MID)
    blocks2 = exchange(fields2)
    field = z_of([pieces0], by_rows[:1], 0, 0, None, HIGH)
    blocks2 = after(blocks2, field)
    (pieces2,) = y_of(blocks2, 1)
    plane = roll_planes(place, (blocks2, 2), (blocks2, 3))
    scalar = by_part(exchange(plane))
    field = z_of([pieces1], by_rows[:1], 1, 0, field)
    field = z_of([pieces2], by_rows[:1], 2, 0, field, HIGH)
    return (field, scalar)


def solution(mesh):
    placed = (P(None, None, None, "ky", "kz"), P())
    return jax.shard_map(
        shards,
        mesh=mesh,
        in_specs=placed,
        out_specs=(P(None, None, "ky", "kz", None), P(None, None, "ky", "kz")),
        check_vma=False,
    )
```
